32 devices in a mesh: tok: 8 (over y, x, core), head: 4 (over z).
Axes of the slice: x: 2, y: 2, z: 4, core: 2. Of those that a mesh axis runs over, the one named last changes fastest.
Arguments:
- fast_query: bfloat16 [2, 1024, 2048], P(None, 'tok', 'head'), may hold values from -6 to 6
- fast_key: bfloat16 [2, 1024, 2048], P(None, 'tok', 'head'), may hold values from -6 to 6
- fast_value: bfloat16 [2, 1024, 2048], P(None, 'tok', 'head'), may hold values from -6 to 6
- fast_rate: float32 [2, 1024, 4], P(None, 'tok', 'head'), may hold values from 0.003125 to 0.03125
- fast_weights: bfloat16 [4, 512, 3, 512], P('head', 'tok'), may hold values from -0.25 to 0.25
- norm_gain: float32 [2048], P('head'), may hold values from 0.25 to 1.75
- key_value: bfloat16 [2, 1024, 512], P(None, 'tok', 'head'), may hold values from -450 to 450
Outputs:
- layer_output: bfloat16 [2, 1024, 2048], P(None, 'tok', 'head')
The draws below stay inside these ranges and needn't reach their ends.
All inputs are finite; a program needn't handle non-finite values.
Results may differ from the reference program's by a relative error of at most 0.04.
The reference program's roundings to bfloat16 on the way count: a program that leaves them out, or rounds other values in their place, can miss the bound.
Values may be sent and summed in bfloat16 or wider, within the bound.
A program may use at most 64 MiB of HBM per device.

```python
import math
import jax
import jax.numpy as jnp
from jax import lax

D = 2048
FWH = 4
HD = 512
FH = 512
QH = 16
KVH = 2
AD = 128
WIN = 1024
BLOCK = 1024


def draw_key_value(key, part):
    key_base = jax.random.fold_in(key, 0)
    key_other = jax.random.fold_in(key, 3)
    columns = 2 * KVH * AD
    column_block = jnp.arange(columns) // AD
    is_key = column_block % 2 == 0
    key_rows = 2.0 * jnp.clip(jax.random.normal(key_base, (2, BLOCK, columns), jnp.float32), -5.0, 5.0)
    value_rows = 3.0 * jnp.clip(jax.random.normal(key_other, (2, BLOCK, columns), jnp.float32), -5.0, 5.0)
    return jnp.where(is_key, key_rows, value_rows).astype(jnp.bfloat16)


def steps_of(stream_key, dims, cuts, smallest, top_value):
    level = 1.0
    for dim, parts in cuts:
        draws = jax.random.uniform(jax.random.fold_in(jax.random.fold_in(stream_key, 6), dim), (parts,), jnp.float32, smallest / len(cuts), top_value / len(cuts))
        level = level * jnp.repeat(jnp.exp(draws), dims[dim] // parts).reshape((-1,) + (1,) * (len(dims) - 1 - dim))
    return level


def gaussian(key, shape, scale, reach, pieces=(), held_as=jnp.bfloat16):
    drawn = scale * jax.random.normal(key, shape, jnp.float32)
    if pieces:
        drawn = drawn * steps_of(key, shape, pieces, -0.22, 0.18)
    return jnp.clip(drawn, -reach, reach).astype(held_as)


def setup_inputs(seed: int = 0) -> dict:
    key_of = jax.random.split(jax.random.key(seed), 8)
    fast_query = gaussian(key_of[0], (2, BLOCK, D), 1.0, 6.0, ((1, 8), (2, 4)))
    fast_key = gaussian(key_of[1], (2, BLOCK, D), 1.0, 6.0, ((1, 8), (2, 4)))
    fast_value = gaussian(key_of[2], (2, BLOCK, D), 1.0, 6.0, ((1, 8), (2, 4)))
    fast_rate = jnp.clip(jnp.exp(math.log(0.03125) - 2.3025851 * jax.random.uniform(key_of[3], (2, BLOCK, FWH), jnp.float32) ** steps_of(key_of[3], (2, BLOCK, FWH), ((1, 8), (2, 4)), -0.2, 0.2)), 0.003125, 0.03125)
    fast_weights = gaussian(key_of[4], (FWH, HD, 3, FH), HD ** -0.5, 0.25, ((0, 4), (1, 8)))
    norm_gain = jnp.clip(1.0 + 0.15 * jax.random.normal(key_of[5], (D,), jnp.float32), 0.25, 1.75)
    key_value = draw_key_value(jax.random.fold_in(key_of[7], 71), 0)
    return {"fast_query": fast_query, "fast_key": fast_key, "fast_value": fast_value, "fast_rate": fast_rate, "fast_weights": fast_weights, "norm_gain": norm_gain, "key_value": key_value}


EPSILON = 1e-06

def fast_apply(inputs, weights):
    gate_value = jnp.dot(inputs, weights[:, 0], preferred_element_type=jnp.float32)
    up_value = jnp.dot(inputs, weights[:, 1], preferred_element_type=jnp.float32)
    hidden = (jax.nn.silu(gate_value) * up_value).astype(jnp.bfloat16)
    return jnp.dot(hidden, weights[:, 2], preferred_element_type=jnp.float32)

def renormed(previous, gradient):
    earlier = previous.astype(jnp.float32)
    updated = earlier + gradient
    factor = jnp.sqrt(lax.optimization_barrier(jnp.mean(earlier * earlier, axis=-1, keepdims=True)) + EPSILON) * lax.rsqrt(lax.optimization_barrier(jnp.mean(updated * updated, axis=-1, keepdims=True)) + EPSILON)
    return (updated * factor).astype(jnp.bfloat16)

def normalized(raw, gain_row):
    factor = lax.rsqrt(lax.optimization_barrier(jnp.mean(raw * raw, axis=-1, keepdims=True)) + EPSILON)
    return (raw * factor * gain_row).astype(jnp.bfloat16)

def head_output(inputs):
    query_in, key_in, value_in, rate_in, weights, gain_row = inputs
    key_first = key_in[0]
    gate_value = jnp.dot(key_first, weights[:, 0], preferred_element_type=jnp.float32)
    up_value = jnp.dot(key_first, weights[:, 1], preferred_element_type=jnp.float32)
    sigmoid_gate = jax.nn.sigmoid(gate_value)
    activated = gate_value * sigmoid_gate
    key_hidden = (activated * up_value).astype(jnp.bfloat16)
    scaled = (rate_in[0] * value_in[0].astype(jnp.float32)).astype(jnp.bfloat16)
    backward = jnp.dot(scaled, weights[:, 2].T, preferred_element_type=jnp.float32)
    gate_grad = (backward * up_value * sigmoid_gate * (1.0 + gate_value * (1.0 - sigmoid_gate))).astype(jnp.bfloat16)
    up_grad = (backward * activated).astype(jnp.bfloat16)
    gradient = jnp.stack([jnp.dot(key_first.T, gate_grad, preferred_element_type=jnp.float32), jnp.dot(key_first.T, up_grad, preferred_element_type=jnp.float32), jnp.dot(key_hidden.T, scaled, preferred_element_type=jnp.float32)], axis=1)
    refreshed = renormed(weights, gradient)
    first_out = normalized(fast_apply(query_in[0], weights), gain_row)
    second_out = normalized(fast_apply(query_in[1], refreshed), gain_row)
    return jnp.stack([first_out, second_out])

def attention_head(queries, key_cols, value_cols):
    total_len = queries.shape[0]
    query_block = min(512, total_len // 2)
    lead = jnp.zeros((WIN, key_cols.shape[1]), key_cols.dtype)
    keys_padded = jnp.concatenate([lead, key_cols], axis=0)
    values_padded = jnp.concatenate([lead, value_cols], axis=0)

    def one_block(block_start):
        query_part = lax.dynamic_slice_in_dim(queries, block_start, query_block, 0)
        key_part = lax.dynamic_slice_in_dim(keys_padded, block_start, query_block + WIN, 0)
        value_part = lax.dynamic_slice_in_dim(values_padded, block_start, query_block + WIN, 0)
        scores = jnp.dot(query_part, key_part.T, preferred_element_type=jnp.float32) / math.sqrt(key_cols.shape[1])
        query_pos = block_start + lax.broadcasted_iota(jnp.int32, scores.shape, 0)
        key_pos = block_start - WIN + lax.broadcasted_iota(jnp.int32, scores.shape, 1)
        offset = query_pos - key_pos
        allowed = (key_pos >= 0) & (offset >= 0) & (offset < WIN)
        scores = jnp.where(allowed, scores, -1e+30)
        row_max = lax.optimization_barrier(jnp.max(scores, axis=-1, keepdims=True))
        lifted = jnp.exp(scores - row_max)
        weights = (lifted / lax.optimization_barrier(jnp.sum(lifted, axis=-1, keepdims=True))).astype(jnp.bfloat16)
        return jnp.dot(weights, value_part, preferred_element_type=jnp.float32)
    starts = jnp.arange(total_len // query_block, dtype=jnp.int32) * query_block
    return lax.map(one_block, starts).reshape(total_len, key_cols.shape[1])

def reference(fast_query, fast_key, fast_value, fast_rate, fast_weights, norm_gain, key_value):

    def split_heads(array):
        return jnp.moveaxis(array.reshape(2, BLOCK, FWH, HD), 2, 0)
    rates = jnp.moveaxis(fast_rate, 2, 0)[..., None]
    gains = norm_gain.reshape(FWH, HD)
    fast_out = lax.map(head_output, (split_heads(fast_query), split_heads(fast_key), split_heads(fast_value), rates, fast_weights, gains))
    fast_out = jnp.moveaxis(fast_out, 0, 2).reshape(2 * BLOCK, D)
    flat_kv = key_value.reshape(2 * BLOCK, 2 * KVH * AD)
    group = QH // KVH

    def one_query_head(head_index):
        queries = lax.dynamic_slice_in_dim(fast_out, (head_index * AD).astype(jnp.int32), AD, 1)
        kv_index = head_index // group
        key_cols = lax.dynamic_slice_in_dim(flat_kv, (2 * kv_index * AD).astype(jnp.int32), AD, 1)
        value_cols = lax.dynamic_slice_in_dim(flat_kv, ((2 * kv_index + 1) * AD).astype(jnp.int32), AD, 1)
        return attention_head(queries, key_cols, value_cols)
    mixed = lax.map(one_query_head, jnp.arange(QH, dtype=jnp.int32))
    attended = jnp.moveaxis(mixed, 0, 1).reshape(2 * BLOCK, D)
    total = (fast_out.astype(jnp.float32) + attended).astype(jnp.bfloat16)
    return total.reshape(2, BLOCK, D)
```

```python
import math

import jax
import jax.numpy as jnp
from jax import lax
from jax.experimental import pallas as pl
from jax.experimental.pallas import tpu as pltpu
from jax.sharding import PartitionSpec as P

WIN = 1024


EPSILON = 1e-06


def from_partner(block, axis, stride):
    count = lax.axis_size(axis)
    route = []
    for low in range(count):
        high = low | 1 << stride
        if high != low and high < count:
            route += [(low, high), (high, low)]
    return lax.ppermute(block, axis, route)


def passed_along(array, axis, by):
    length = lax.axis_size(axis)
    return lax.ppermute(array, axis, [(i, (i + by) % length) for i in range(length)])


def product(inputs, matrix):
    return jnp.dot(inputs, matrix, preferred_element_type=jnp.float32)


def fast_apply(inputs, weights):
    gate_value = product(inputs, weights[:, 0])
    up_value = product(inputs, weights[:, 1])
    hidden = (jax.nn.silu(gate_value) * up_value).astype(jnp.bfloat16)
    return product(hidden, weights[:, 2])


def backward_terms(key_in, value_in, rates, weights):
    gate_value = product(key_in, weights[:, 0])
    up_value = product(key_in, weights[:, 1])
    sigmoid_gate = jax.nn.sigmoid(gate_value)
    activated = gate_value * sigmoid_gate
    key_hidden = (activated * up_value).astype(jnp.bfloat16)
    scaled = (rates * value_in.astype(jnp.float32)).astype(jnp.bfloat16)
    backward = lax.dot_general(
        scaled, weights[:, 2], (((1,), (1,)), ((), ())), preferred_element_type=jnp.float32
    )
    gate_grad = (
        backward * up_value * sigmoid_gate * (1.0 + gate_value * (1.0 - sigmoid_gate))
    ).astype(jnp.bfloat16)
    up_grad = (backward * activated).astype(jnp.bfloat16)
    return (key_hidden, scaled, gate_grad, up_grad)


def gradient_rows(key_in, terms):
    key_hidden, scaled, gate_grad, up_grad = terms
    across = (((0,), (0,)), ((), ()))
    gate_rows = lax.dot_general(key_in, gate_grad, across, preferred_element_type=jnp.float32)
    up_rows = lax.dot_general(key_in, up_grad, across, preferred_element_type=jnp.float32)
    down_rows = lax.dot_general(key_hidden, scaled, across, preferred_element_type=jnp.float32)
    return jnp.stack([gate_rows, up_rows, down_rows], axis=1)


def renormed(previous, gradient):
    earlier = previous.astype(jnp.float32)
    updated = earlier + gradient
    factor = jnp.sqrt(jnp.mean(earlier * earlier, axis=-1, keepdims=True) + EPSILON) * lax.rsqrt(
        jnp.mean(updated * updated, axis=-1, keepdims=True) + EPSILON
    )
    return (updated * factor).astype(jnp.bfloat16)


def normalized(raw, gain_row):
    factor = lax.rsqrt(jnp.mean(raw * raw, axis=-1, keepdims=True) + EPSILON)
    return (raw * factor * gain_row).astype(jnp.bfloat16)


def attend(queries, key_block, value_block, allowed, head_size):
    tokens = queries.shape[0]
    per_head = queries.reshape(tokens, -1, head_size)
    scores = jnp.einsum(
        "qhd,kd->hqk", per_head, key_block, preferred_element_type=jnp.float32
    ) / math.sqrt(head_size)
    scores = jnp.where(allowed[None], scores, -1e30)
    row_max = jnp.max(scores, axis=-1, keepdims=True)
    lifted = jnp.exp(scores - row_max)
    weights = (lifted / jnp.sum(lifted, axis=-1, keepdims=True)).astype(jnp.bfloat16)
    mixed = jnp.einsum("hqk,kd->qhd", weights, value_block, preferred_element_type=jnp.float32)
    return mixed.reshape(tokens, -1)


def shards(fast_query, fast_key, fast_value, fast_rate, fast_weights, norm_gain, key_value):
    tokens = fast_query.shape[1]
    head_size = key_value.shape[2]
    place = lax.axis_index("tok")
    block_len = tokens * lax.axis_size("tok")
    own_rows = fast_weights[0]
    initial = lax.all_gather(own_rows, "tok", axis=0, tiled=True)
    terms = backward_terms(fast_key[0], fast_value[0], fast_rate[0], initial)
    gradient = lax.psum(gradient_rows(fast_key[0], terms), "tok")
    refreshed = renormed(initial, gradient)
    partner = from_partner(key_value, "head", 0)
    holds_key = lax.axis_index("head") % 2 == 0
    key_part = jnp.where(holds_key, key_value, partner)
    value_part = jnp.where(holds_key, partner, key_value)
    pair_stack = jnp.stack([key_part, value_part])
    reach = WIN // tokens
    arrived = []
    for distance in range(1, reach + 1):
        arrived.append(passed_along(pair_stack, "tok", distance))
    aligned = []
    for distance in range(reach, 0, -1):
        piece = arrived[distance - 1]
        aligned.append(jnp.where(place >= distance, piece, piece[:, 0:1]))
    aligned.append(pair_stack)
    window = jnp.concatenate(aligned, axis=2)
    span = window.shape[2]
    query_pos = lax.broadcasted_iota(jnp.int32, (tokens, span), 0)
    key_pos = lax.broadcasted_iota(jnp.int32, (tokens, span), 1) - reach * tokens
    offset = query_pos - key_pos
    inside = (offset >= 0) & (offset < WIN)

    def finish(block_index, matrices):
        fast_out = normalized(fast_apply(fast_query[block_index], matrices), norm_gain)
        allowed = inside & (block_index * block_len + place * tokens + key_pos >= 0)
        attended = attend(
            fast_out, window[0, block_index], window[1, block_index], allowed, head_size
        )
        return (fast_out.astype(jnp.float32) + attended).astype(jnp.bfloat16)

    first_final = finish(0, initial)
    second_final = finish(1, refreshed)
    return jnp.stack([first_final, second_final])

MESH = pl.DeviceIdType.MESH
ALONG_ROWS = (((0,), (0,)), ((), ()))
ALONG_COLUMNS = (((1,), (1,)), ((), ()))


def dot_along(left, right, dims):
    return lax.dot_general(left, right, dims, preferred_element_type=jnp.float32)


def mixed_heads(fast_out, keys, values, valid):
    tokens = fast_out.shape[0]
    size = keys[0].shape[1]
    heads = fast_out.shape[1] // size
    stacked = jnp.concatenate([fast_out[:, h * size : (h + 1) * size] for h in range(heads)], axis=0)
    scale = math.log2(math.e) / math.sqrt(size)
    scores = [dot_along(stacked, part, ALONG_COLUMNS) for part in keys]
    pieces = []
    for h in range(heads):
        masked = [
            jnp.where(ok, s[h * tokens : (h + 1) * tokens], -1e30) for s, ok in zip(scores, valid)
        ]
        top = jnp.max(masked[0], axis=-1, keepdims=True)
        for more in masked[1:]:
            top = jnp.maximum(top, jnp.max(more, axis=-1, keepdims=True))
        lifted = [jnp.exp2((part - top) * scale) for part in masked]
        total = jnp.sum(lifted[0], axis=-1, keepdims=True)
        for more in lifted[1:]:
            total = total + jnp.sum(more, axis=-1, keepdims=True)
        inverse = 1.0 / total
        pieces.append([(part * inverse).astype(jnp.bfloat16) for part in lifted])
    mixed = None
    for i, part in enumerate(values):
        weights = jnp.concatenate([piece[i] for piece in pieces], axis=0)
        term = product(weights, part)
        mixed = term if mixed is None else mixed + term
    return jnp.concatenate([mixed[h * tokens : (h + 1) * tokens] for h in range(heads)], axis=1)


def whole_kernel(
    query_ref, key_ref, value_ref, rate_ref, weight_ref, gain_ref, kv_ref, out_ref,
    w_buf, k_buf, s_buf, kv_buf, hidden_buf, gates_buf, new_buf, merged,
    send_sem, recv_sem, z_send, z_recv,
):
    me = lax.axis_index("tok")
    head = lax.axis_index("head")
    kind = lax.rem(head, 2)
    core = lax.rem(me, 2)
    first_hop = jnp.where(core == 0, 2, 4)
    second_hop = 6 - first_hop
    sibling = me ^ 1
    near, far = me ^ first_hop, me ^ second_hop
    opposite = me ^ 6
    opposite_head = head ^ 1
    barrier = pltpu.get_barrier_semaphore()
    for there in (sibling, near, far):
        pl.semaphore_signal(barrier, inc=1, device_id=(there, head), device_id_type=MESH)
    pl.semaphore_signal(barrier, inc=1, device_id=(me, opposite_head), device_id_type=MESH)

    tokens = key_ref.shape[1]
    depth = weight_ref.shape[0]
    hd = key_ref.shape[2]
    size = kv_ref.shape[2]

    def rows(owner, count):
        return pl.ds(pl.multiple_of(owner * count, count), count)

    own = rows(me, tokens)
    w_buf[rows(me, depth)] = weight_ref[...]
    k_buf[own] = key_ref[0]
    s_buf[own] = (rate_ref[0] * value_ref[0].astype(jnp.float32)).astype(jnp.bfloat16)
    kv_buf[kind, :, own] = kv_ref[...]

    def part_of(item, owner):
        if item == 0:
            return w_buf.at[rows(owner, depth)]
        if item == 1:
            return kv_buf.at[kind, :, rows(owner, tokens)]
        if item == 2:
            return k_buf.at[rows(owner, tokens)]
        if item == 3:
            return s_buf.at[rows(owner, tokens)]
        return kv_buf.at[1 - kind, :, rows(owner, tokens)]

    owners = [
        me, near, far, opposite,
        sibling, sibling ^ 2, sibling ^ 4, sibling ^ 6,
    ]
    started = []

    def send(item, source, target, slot):
        number = len(started)
        copy = pltpu.make_async_remote_copy(
            src_ref=part_of(item, owners[source]),
            dst_ref=part_of(item, owners[source]),
            send_sem=send_sem.at[number],
            recv_sem=recv_sem.at[item, slot],
            device_id=(target, head),
            device_id_type=MESH,
        )
        copy.start()
        started.append(copy)

    across = []

    def send_across(source):
        ref = part_of(1, owners[source])
        copy = pltpu.make_async_remote_copy(
            src_ref=ref, dst_ref=ref, send_sem=z_send.at[source], recv_sem=z_recv.at[source],
            device_id=(me, opposite_head), device_id_type=MESH,
        )
        copy.start()
        across.append(copy)

    def arrived(item, slot):
        ref = part_of(item, owners[slot])
        pltpu.make_async_remote_copy(
            src_ref=ref, dst_ref=ref, send_sem=send_sem.at[0], recv_sem=recv_sem.at[item, slot],
            device_id=(sibling, head), device_id_type=MESH,
        ).wait_recv()

    def arrived_across(source):
        ref = part_of(4, owners[source])
        pltpu.make_async_remote_copy(
            src_ref=ref, dst_ref=ref, send_sem=z_send.at[0], recv_sem=z_recv.at[source],
            device_id=(me, opposite_head), device_id_type=MESH,
        ).wait_recv()

    side = {0: 4, 1: jnp.where(core == 0, 5, 6), 2: jnp.where(core == 0, 6, 5), 3: 7}

    def to_sibling(item, source):
        send(item, source, sibling, side[source])

    def pass_on(item, source):
        arrived(item, source)
        if source == 1:
            send(item, 1, far, 3)
        to_sibling(item, source)

    pl.semaphore_wait(barrier, 4)
    for item in (0, 1, 2, 3):
        send(item, 0, near, 1)
        send(item, 0, far, 2)
        to_sibling(item, 0)
        if item == 1:
            send_across(0)

    pass_on(0, 1)
    pass_on(0, 2)
    pass_on(1, 1)
    send_across(1)
    pass_on(1, 2)
    send_across(2)
    pass_on(0, 3)
    for slot in range(4, 8):
        arrived(0, slot)

    gain = gain_ref[...]

    def rms(total):
        return lax.rsqrt(jnp.mean(total * total, axis=-1, keepdims=True) + EPSILON)

    def applied(block, buf):
        both = product(query_ref[block], buf[:, : 2 * hd])
        gate_value, up_value = both[:, :hd], both[:, hd:]
        hidden = (jax.nn.silu(gate_value) * up_value).astype(jnp.bfloat16)
        raw = product(hidden, buf[:, 2 * hd :])
        return (raw * rms(raw) * gain).astype(jnp.bfloat16)

    fast_first = applied(0, w_buf)

    def terms(chip):
        span = rows(chip, 2 * tokens)
        both = product(k_buf[span], w_buf[:, : 2 * hd])
        gate_value, up_value = both[:, :hd], both[:, hd:]
        sig = jax.nn.sigmoid(gate_value)
        act = gate_value * sig
        hidden_buf[span] = (act * up_value).astype(jnp.bfloat16)
        backward = dot_along(s_buf[span], w_buf[:, 2 * hd :], ALONG_COLUMNS)
        gates_buf[span, :hd] = (
            backward * up_value * sig * (1.0 + gate_value * (1.0 - sig))
        ).astype(jnp.bfloat16)
        gates_buf[span, hd:] = (backward * act).astype(jnp.bfloat16)

    chip = me // 2
    arrived(2, 4)
    arrived(3, 4)
    pass_on(2, 1)
    pass_on(3, 1)
    terms(chip)
    pass_on(2, 2)
    pass_on(3, 2)
    pass_on(1, 3)
    send_across(3)
    for source in range(4):
        arrived_across(source)
        to_sibling(4, source)
    for slot in (5, 6):
        arrived(2, slot)
        arrived(3, slot)
    terms(chip ^ 1)
    terms(chip ^ 2)
    for slot in range(4, 8):
        arrived(1, slot)
        arrived(4, slot)
    pass_on(2, 3)
    pass_on(3, 3)

    length = k_buf.shape[0]
    query_pos = me * tokens + lax.broadcasted_iota(jnp.int32, (tokens, length), 0)
    key_pos = lax.broadcasted_iota(jnp.int32, (tokens, length), 1)
    mixed = mixed_heads(fast_first, [kv_buf[0, 0]], [kv_buf[1, 0]], [key_pos <= query_pos])
    out_ref[0] = (fast_first.astype(jnp.float32) + mixed).astype(jnp.bfloat16)

    arrived(2, 7)
    arrived(3, 7)
    terms(chip ^ 3)

    def renewed(part, gradient):
        columns = slice(part * hd, (part + 1) * hd)
        earlier = w_buf[:, columns].astype(jnp.float32)
        updated = earlier + gradient
        factor = jnp.sqrt(jnp.mean(earlier * earlier, axis=-1, keepdims=True) + EPSILON) * rms(updated)
        new_buf[:, columns] = (updated * factor).astype(jnp.bfloat16)

    both = dot_along(k_buf[...], gates_buf[...], ALONG_ROWS)
    renewed(0, both[:, :hd])
    renewed(1, both[:, hd:])
    renewed(2, dot_along(hidden_buf[...], s_buf[...], ALONG_ROWS))

    fast_second = applied(1, new_buf)
    for shard in range(length // tokens):
        place = slice(shard * tokens, (shard + 1) * tokens)
        block = jnp.where(shard < me, 1, 0)
        merged[0, place] = kv_buf[0, block, place]
        merged[1, place] = kv_buf[1, block, place]
    near_query = lax.broadcasted_iota(jnp.int32, (tokens, tokens), 0)
    near_key = lax.broadcasted_iota(jnp.int32, (tokens, tokens), 1)
    mixed = mixed_heads(
        fast_second,
        [merged[0], kv_buf[0, 1, own]],
        [merged[1], kv_buf[1, 1, own]],
        [(key_pos < me * tokens) | (key_pos > query_pos), near_key <= near_query],
    )
    out_ref[1] = (fast_second.astype(jnp.float32) + mixed).astype(jnp.bfloat16)
    for copy in started + across:
        copy.wait_send()


def gathered_shards(fast_query, fast_key, fast_value, fast_rate, fast_weights, norm_gain, key_value):
    members = lax.axis_size("tok")
    _, depth, parts, hd = fast_weights.shape
    _, tokens, size = key_value.shape
    length = members * tokens
    weights = fast_weights[0].reshape(depth, parts * hd)
    sends = 4 * (members - 1) + members // 2
    bf16 = jnp.bfloat16
    return pl.pallas_call(
        whole_kernel,
        out_shape=jax.ShapeDtypeStruct(fast_query.shape, bf16),
        in_specs=[pl.BlockSpec(memory_space=pltpu.VMEM)] * 7,
        out_specs=pl.BlockSpec(memory_space=pltpu.VMEM),
        scratch_shapes=[
            pltpu.VMEM((members * depth, parts * hd), bf16),
            pltpu.VMEM((length, hd), bf16),
            pltpu.VMEM((length, hd), bf16),
            pltpu.VMEM((2, 2, length, size), bf16),
            pltpu.VMEM((length, hd), bf16),
            pltpu.VMEM((length, 2 * hd), bf16),
            pltpu.VMEM((members * depth, parts * hd), bf16),
            pltpu.VMEM((2, length, size), bf16),
            pltpu.SemaphoreType.DMA((sends,)),
            pltpu.SemaphoreType.DMA((5, members)),
            pltpu.SemaphoreType.DMA((members // 2,)),
            pltpu.SemaphoreType.DMA((members // 2,)),
        ],
        compiler_params=pltpu.CompilerParams(
            collective_id=0, has_side_effects=True, vmem_limit_bytes=56 * 1024 * 1024
        ),
    )(fast_query, fast_key, fast_value, fast_rate, weights, norm_gain[None], key_value)


def solution(mesh):
    in_specs = (
        P(None, "tok", "head"),
        P(None, "tok", "head"),
        P(None, "tok", "head"),
        P(None, "tok", "head"),
        P("head", "tok", None, None),
        P("head"),
        P(None, "tok", "head"),
    )
    out_specs = P(None, "tok", "head")
    plan = gathered_shards if mesh.shape["tok"] == 8 else shards
    return jax.shard_map(plan, mesh=mesh, in_specs=in_specs, out_specs=out_specs, check_vma=False)
```

```python
import math

import jax
import jax.numpy as jnp
from jax import lax
from jax.experimental import pallas as pl
from jax.experimental.pallas import tpu as pltpu
from jax.sharding import PartitionSpec as P

WIN = 1024


EPSILON = 1e-06


def from_partner(block, axis, stride):
    count = lax.axis_size(axis)
    route = []
    for low in range(count):
        high = low | 1 << stride
        if high != low and high < count:
            route += [(low, high), (high, low)]
    return lax.ppermute(block, axis, route)


def passed_along(array, axis, by):
    length = lax.axis_size(axis)
    return lax.ppermute(array, axis, [(i, (i + by) % length) for i in range(length)])


def product(inputs, matrix):
    return jnp.dot(inputs, matrix, preferred_element_type=jnp.float32)


def fast_apply(inputs, weights):
    gate_value = product(inputs, weights[:, 0])
    up_value = product(inputs, weights[:, 1])
    hidden = (jax.nn.silu(gate_value) * up_value).astype(jnp.bfloat16)
    return product(hidden, weights[:, 2])


def backward_terms(key_in, value_in, rates, weights):
    gate_value = product(key_in, weights[:, 0])
    up_value = product(key_in, weights[:, 1])
    sigmoid_gate = jax.nn.sigmoid(gate_value)
    activated = gate_value * sigmoid_gate
    key_hidden = (activated * up_value).astype(jnp.bfloat16)
    scaled = (rates * value_in.astype(jnp.float32)).astype(jnp.bfloat16)
    backward = lax.dot_general(
        scaled, weights[:, 2], (((1,), (1,)), ((), ())), preferred_element_type=jnp.float32
    )
    gate_grad = (
        backward * up_value * sigmoid_gate * (1.0 + gate_value * (1.0 - sigmoid_gate))
    ).astype(jnp.bfloat16)
    up_grad = (backward * activated).astype(jnp.bfloat16)
    return (key_hidden, scaled, gate_grad, up_grad)


def gradient_rows(key_in, terms):
    key_hidden, scaled, gate_grad, up_grad = terms
    across = (((0,), (0,)), ((), ()))
    gate_rows = lax.dot_general(key_in, gate_grad, across, preferred_element_type=jnp.float32)
    up_rows = lax.dot_general(key_in, up_grad, across, preferred_element_type=jnp.float32)
    down_rows = lax.dot_general(key_hidden, scaled, across, preferred_element_type=jnp.float32)
    return jnp.stack([gate_rows, up_rows, down_rows], axis=1)


def renormed(previous, gradient):
    earlier = previous.astype(jnp.float32)
    updated = earlier + gradient
    factor = jnp.sqrt(jnp.mean(earlier * earlier, axis=-1, keepdims=True) + EPSILON) * lax.rsqrt(
        jnp.mean(updated * updated, axis=-1, keepdims=True) + EPSILON
    )
    return (updated * factor).astype(jnp.bfloat16)


def normalized(raw, gain_row):
    factor = lax.rsqrt(jnp.mean(raw * raw, axis=-1, keepdims=True) + EPSILON)
    return (raw * factor * gain_row).astype(jnp.bfloat16)


def attend(queries, key_block, value_block, allowed, head_size):
    tokens = queries.shape[0]
    per_head = queries.reshape(tokens, -1, head_size)
    scores = jnp.einsum(
        "qhd,kd->hqk", per_head, key_block, preferred_element_type=jnp.float32
    ) / math.sqrt(head_size)
    scores = jnp.where(allowed[None], scores, -1e30)
    row_max = jnp.max(scores, axis=-1, keepdims=True)
    lifted = jnp.exp(scores - row_max)
    weights = (lifted / jnp.sum(lifted, axis=-1, keepdims=True)).astype(jnp.bfloat16)
    mixed = jnp.einsum("hqk,kd->qhd", weights, value_block, preferred_element_type=jnp.float32)
    return mixed.reshape(tokens, -1)


def shards(fast_query, fast_key, fast_value, fast_rate, fast_weights, norm_gain, key_value):
    tokens = fast_query.shape[1]
    head_size = key_value.shape[2]
    place = lax.axis_index("tok")
    block_len = tokens * lax.axis_size("tok")
    own_rows = fast_weights[0]
    initial = lax.all_gather(own_rows, "tok", axis=0, tiled=True)
    terms = backward_terms(fast_key[0], fast_value[0], fast_rate[0], initial)
    gradient = lax.psum(gradient_rows(fast_key[0], terms), "tok")
    refreshed = renormed(initial, gradient)
    partner = from_partner(key_value, "head", 0)
    holds_key = lax.axis_index("head") % 2 == 0
    key_part = jnp.where(holds_key, key_value, partner)
    value_part = jnp.where(holds_key, partner, key_value)
    pair_stack = jnp.stack([key_part, value_part])
    reach = WIN // tokens
    arrived = []
    for distance in range(1, reach + 1):
        arrived.append(passed_along(pair_stack, "tok", distance))
    aligned = []
    for distance in range(reach, 0, -1):
        piece = arrived[distance - 1]
        aligned.append(jnp.where(place >= distance, piece, piece[:, 0:1]))
    aligned.append(pair_stack)
    window = jnp.concatenate(aligned, axis=2)
    span = window.shape[2]
    query_pos = lax.broadcasted_iota(jnp.int32, (tokens, span), 0)
    key_pos = lax.broadcasted_iota(jnp.int32, (tokens, span), 1) - reach * tokens
    offset = query_pos - key_pos
    inside = (offset >= 0) & (offset < WIN)

    def finish(block_index, matrices):
        fast_out = normalized(fast_apply(fast_query[block_index], matrices), norm_gain)
        allowed = inside & (block_index * block_len + place * tokens + key_pos >= 0)
        attended = attend(
            fast_out, window[0, block_index], window[1, block_index], allowed, head_size
        )
        return (fast_out.astype(jnp.float32) + attended).astype(jnp.bfloat16)

    first_final = finish(0, initial)
    second_final = finish(1, refreshed)
    return jnp.stack([first_final, second_final])

MESH = pl.DeviceIdType.MESH
ALONG_ROWS = (((0,), (0,)), ((), ()))
ALONG_COLUMNS = (((1,), (1,)), ((), ()))


def dot_along(left, right, dims):
    return lax.dot_general(left, right, dims, preferred_element_type=jnp.float32)


def mixed_heads(fast_out, keys, values, valid):
    tokens = fast_out.shape[0]
    size = keys[0].shape[1]
    heads = fast_out.shape[1] // size
    stacked = jnp.concatenate([fast_out[:, h * size : (h + 1) * size] for h in range(heads)], axis=0)
    scale = math.log2(math.e) / math.sqrt(size)
    scores = [dot_along(stacked, part, ALONG_COLUMNS) for part in keys]
    pieces = []
    for h in range(heads):
        masked = [
            jnp.where(ok, s[h * tokens : (h + 1) * tokens], -1e30) for s, ok in zip(scores, valid)
        ]
        top = jnp.max(masked[0], axis=-1, keepdims=True)
        for more in masked[1:]:
            top = jnp.maximum(top, jnp.max(more, axis=-1, keepdims=True))
        lifted = [jnp.exp2((part - top) * scale) for part in masked]
        total = jnp.sum(lifted[0], axis=-1, keepdims=True)
        for more in lifted[1:]:
            total = total + jnp.sum(more, axis=-1, keepdims=True)
        inverse = 1.0 / total
        pieces.append([(part * inverse).astype(jnp.bfloat16) for part in lifted])
    mixed = None
    for i, part in enumerate(values):
        weights = jnp.concatenate([piece[i] for piece in pieces], axis=0)
        term = product(weights, part)
        mixed = term if mixed is None else mixed + term
    return jnp.concatenate([mixed[h * tokens : (h + 1) * tokens] for h in range(heads)], axis=1)


def whole_kernel(
    query_ref, key_ref, value_ref, rate_ref, weight_ref, gain_ref, kv_ref, out_ref,
    w_buf, k_buf, s_buf, kv_buf, hidden_buf, gates_buf, new_buf, merged,
    send_sem, recv_sem, z_send, z_recv,
):
    me = lax.axis_index("tok")
    head = lax.axis_index("head")
    kind = lax.rem(head, 2)
    core = lax.rem(me, 2)
    first_hop = jnp.where(core == 0, 2, 4)
    second_hop = 6 - first_hop
    sibling = me ^ 1
    near, far = me ^ first_hop, me ^ second_hop
    opposite = me ^ 6
    opposite_head = head ^ 1
    barrier = pltpu.get_barrier_semaphore()
    for there in (sibling, near, far):
        pl.semaphore_signal(barrier, inc=1, device_id=(there, head), device_id_type=MESH)
    pl.semaphore_signal(barrier, inc=1, device_id=(me, opposite_head), device_id_type=MESH)

    tokens = key_ref.shape[1]
    parts, depth, _ = weight_ref.shape
    hd = key_ref.shape[2]
    size = kv_ref.shape[2]

    def rows(owner, count):
        return pl.ds(pl.multiple_of(owner * count, count), count)

    own = rows(me, tokens)
    for part in range(parts):
        w_buf[rows(me, depth), part * hd : (part + 1) * hd] = weight_ref[part]
    k_buf[own] = key_ref[0]
    rates = jnp.broadcast_to(rate_ref[0], (tokens, tokens)).T[:, :1]
    s_buf[own] = (rates * value_ref[0].astype(jnp.float32)).astype(jnp.bfloat16)
    kv_buf[kind, :, own] = kv_ref[...]

    def part_of(item, owner):
        if item == 0:
            return w_buf.at[rows(owner, depth)]
        if item == 1:
            return kv_buf.at[kind, :, rows(owner, tokens)]
        if item == 2:
            return k_buf.at[rows(owner, tokens)]
        if item == 3:
            return s_buf.at[rows(owner, tokens)]
        return kv_buf.at[1 - kind, :, rows(owner, tokens)]

    owners = [
        me, near, far, opposite,
        sibling, sibling ^ 2, sibling ^ 4, sibling ^ 6,
    ]
    started = []

    def send(item, source, target, slot):
        number = len(started)
        copy = pltpu.make_async_remote_copy(
            src_ref=part_of(item, owners[source]),
            dst_ref=part_of(item, owners[source]),
            send_sem=send_sem.at[number],
            recv_sem=recv_sem.at[item, slot],
            device_id=(target, head),
            device_id_type=MESH,
        )
        copy.start()
        started.append(copy)

    across = []

    def send_across(source):
        ref = part_of(1, owners[source])
        copy = pltpu.make_async_remote_copy(
            src_ref=ref, dst_ref=ref, send_sem=z_send.at[source], recv_sem=z_recv.at[source],
            device_id=(me, opposite_head), device_id_type=MESH,
        )
        copy.start()
        across.append(copy)

    def arrived(item, slot):
        ref = part_of(item, owners[slot])
        pltpu.make_async_remote_copy(
            src_ref=ref, dst_ref=ref, send_sem=send_sem.at[0], recv_sem=recv_sem.at[item, slot],
            device_id=(sibling, head), device_id_type=MESH,
        ).wait_recv()

    def arrived_across(source):
        ref = part_of(4, owners[source])
        pltpu.make_async_remote_copy(
            src_ref=ref, dst_ref=ref, send_sem=z_send.at[0], recv_sem=z_recv.at[source],
            device_id=(me, opposite_head), device_id_type=MESH,
        ).wait_recv()

    side = {0: 4, 1: jnp.where(core == 0, 5, 6), 2: jnp.where(core == 0, 6, 5), 3: 7}

    def to_sibling(item, source):
        send(item, source, sibling, side[source])

    def pass_on(item, source):
        arrived(item, source)
        if source == 1:
            send(item, 1, far, 3)
        to_sibling(item, source)

    pl.semaphore_wait(barrier, 4)
    for item in range(4):
        send(item, 0, near, 1)
    for item in range(2):
        send(item, 0, far, 2)
    for item in range(4):
        to_sibling(item, 0)
    send_across(0)
    for item in range(4):
        pass_on(item, 1)
        if item < 2:
            send(item + 2, 0, far, 2)
        if item == 1:
            send_across(1)
    pass_on(0, 2)
    pass_on(1, 2)
    send_across(2)
    pass_on(2, 2)
    pass_on(0, 3)
    for slot in range(4, 8):
        arrived(0, slot)

    gain = gain_ref[...]

    def rms(total):
        return lax.rsqrt(jnp.mean(total * total, axis=-1, keepdims=True) + EPSILON)

    def applied(block, buf):
        both = product(query_ref[block], buf[:, : 2 * hd])
        gate_value, up_value = both[:, :hd], both[:, hd:]
        hidden = (jax.nn.silu(gate_value) * up_value).astype(jnp.bfloat16)
        raw = product(hidden, buf[:, 2 * hd :])
        return (raw * rms(raw) * gain).astype(jnp.bfloat16)

    fast_first = applied(0, w_buf)

    def terms(chip):
        span = rows(chip, 2 * tokens)
        both = product(k_buf[span], w_buf[:, : 2 * hd])
        gate_value, up_value = both[:, :hd], both[:, hd:]
        sig = jax.nn.sigmoid(gate_value)
        act = gate_value * sig
        hidden_buf[span] = (act * up_value).astype(jnp.bfloat16)
        backward = dot_along(s_buf[span], w_buf[:, 2 * hd :], ALONG_COLUMNS)
        gates_buf[span, :hd] = (
            backward * up_value * sig * (1.0 + gate_value * (1.0 - sig))
        ).astype(jnp.bfloat16)
        gates_buf[span, hd:] = (backward * act).astype(jnp.bfloat16)

    chip = me // 2
    arrived(2, 4)
    arrived(3, 4)
    terms(chip)
    pass_on(3, 2)
    pass_on(1, 3)
    send_across(3)
    for source in range(4):
        arrived_across(source)
        to_sibling(4, source)
    for slot in (5, 6):
        arrived(2, slot)
        arrived(3, slot)
    terms(chip ^ 1)
    terms(chip ^ 2)
    for slot in range(4, 8):
        arrived(1, slot)
        arrived(4, slot)
    pass_on(2, 3)
    pass_on(3, 3)

    length = k_buf.shape[0]
    query_pos = me * tokens + lax.broadcasted_iota(jnp.int32, (tokens, length), 0)
    key_pos = lax.broadcasted_iota(jnp.int32, (tokens, length), 1)
    mixed = mixed_heads(fast_first, [kv_buf[0, 0]], [kv_buf[1, 0]], [key_pos <= query_pos])
    out_ref[0] = (fast_first.astype(jnp.float32) + mixed).astype(jnp.bfloat16)

    arrived(2, 7)
    arrived(3, 7)
    terms(chip ^ 3)

    def renewed(part, gradient):
        columns = slice(part * hd, (part + 1) * hd)
        earlier = w_buf[:, columns].astype(jnp.float32)
        updated = earlier + gradient
        factor = jnp.sqrt(jnp.mean(earlier * earlier, axis=-1, keepdims=True) + EPSILON) * rms(updated)
        new_buf[:, columns] = (updated * factor).astype(jnp.bfloat16)

    both = dot_along(k_buf[...], gates_buf[...], ALONG_ROWS)
    renewed(0, both[:, :hd])
    renewed(1, both[:, hd:])
    renewed(2, dot_along(hidden_buf[...], s_buf[...], ALONG_ROWS))

    fast_second = applied(1, new_buf)
    for shard in range(length // tokens):
        place = slice(shard * tokens, (shard + 1) * tokens)
        block = jnp.where(shard < me, 1, 0)
        merged[0, place] = kv_buf[0, block, place]
        merged[1, place] = kv_buf[1, block, place]
    near_query = lax.broadcasted_iota(jnp.int32, (tokens, tokens), 0)
    near_key = lax.broadcasted_iota(jnp.int32, (tokens, tokens), 1)
    mixed = mixed_heads(
        fast_second,
        [merged[0], kv_buf[0, 1, own]],
        [merged[1], kv_buf[1, 1, own]],
        [(key_pos < me * tokens) | (key_pos > query_pos), near_key <= near_query],
    )
    out_ref[1] = (fast_second.astype(jnp.float32) + mixed).astype(jnp.bfloat16)
    for copy in started + across:
        copy.wait_send()


def gathered_shards(fast_query, fast_key, fast_value, fast_rate, fast_weights, norm_gain, key_value):
    members = lax.axis_size("tok")
    _, depth, parts, hd = fast_weights.shape
    _, tokens, size = key_value.shape
    length = members * tokens
    weights = jnp.swapaxes(fast_weights[0], 0, 1)
    rates = jnp.swapaxes(fast_rate, 1, 2)
    sends = 4 * (members - 1) + members // 2
    bf16 = jnp.bfloat16
    return pl.pallas_call(
        whole_kernel,
        out_shape=jax.ShapeDtypeStruct(fast_query.shape, bf16),
        in_specs=[pl.BlockSpec(memory_space=pltpu.VMEM)] * 7,
        out_specs=pl.BlockSpec(memory_space=pltpu.VMEM),
        scratch_shapes=[
            pltpu.VMEM((members * depth, parts * hd), bf16),
            pltpu.VMEM((length, hd), bf16),
            pltpu.VMEM((length, hd), bf16),
            pltpu.VMEM((2, 2, length, size), bf16),
            pltpu.VMEM((length, hd), bf16),
            pltpu.VMEM((length, 2 * hd), bf16),
            pltpu.VMEM((members * depth, parts * hd), bf16),
            pltpu.VMEM((2, length, size), bf16),
            pltpu.SemaphoreType.DMA((sends,)),
            pltpu.SemaphoreType.DMA((5, members)),
            pltpu.SemaphoreType.DMA((members // 2,)),
            pltpu.SemaphoreType.DMA((members // 2,)),
        ],
        compiler_params=pltpu.CompilerParams(
            collective_id=0, has_side_effects=True, vmem_limit_bytes=60 * 1024 * 1024
        ),
    )(fast_query, fast_key, fast_value, rates, weights, norm_gain[None], key_value)


def solution(mesh):
    in_specs = (
        P(None, "tok", "head"),
        P(None, "tok", "head"),
        P(None, "tok", "head"),
        P(None, "tok", "head"),
        P("head", "tok", None, None),
        P("head"),
        P(None, "tok", "head"),
    )
    out_specs = P(None, "tok", "head")
    plan = gathered_shards if mesh.shape["tok"] == 8 else shards
    return jax.shard_map(plan, mesh=mesh, in_specs=in_specs, out_specs=out_specs, check_vma=False)
```

```python
import math

import jax
import jax.numpy as jnp
from jax import lax
from jax.experimental import pallas as pl
from jax.experimental.pallas import tpu as pltpu
from jax.sharding import PartitionSpec as P

WIN = 1024


EPSILON = 1e-06


def from_partner(block, axis, stride):
    count = lax.axis_size(axis)
    route = []
    for low in range(count):
        high = low | 1 << stride
        if high != low and high < count:
            route += [(low, high), (high, low)]
    return lax.ppermute(block, axis, route)


def passed_along(array, axis, by):
    length = lax.axis_size(axis)
    return lax.ppermute(array, axis, [(i, (i + by) % length) for i in range(length)])


def product(inputs, matrix):
    return jnp.dot(inputs, matrix, preferred_element_type=jnp.float32)


def fast_apply(inputs, weights):
    gate_value = product(inputs, weights[:, 0])
    up_value = product(inputs, weights[:, 1])
    hidden = (jax.nn.silu(gate_value) * up_value).astype(jnp.bfloat16)
    return product(hidden, weights[:, 2])


def backward_terms(key_in, value_in, rates, weights):
    gate_value = product(key_in, weights[:, 0])
    up_value = product(key_in, weights[:, 1])
    sigmoid_gate = jax.nn.sigmoid(gate_value)
    activated = gate_value * sigmoid_gate
    key_hidden = (activated * up_value).astype(jnp.bfloat16)
    scaled = (rates * value_in.astype(jnp.float32)).astype(jnp.bfloat16)
    backward = lax.dot_general(
        scaled, weights[:, 2], (((1,), (1,)), ((), ())), preferred_element_type=jnp.float32
    )
    gate_grad = (
        backward * up_value * sigmoid_gate * (1.0 + gate_value * (1.0 - sigmoid_gate))
    ).astype(jnp.bfloat16)
    up_grad = (backward * activated).astype(jnp.bfloat16)
    return (key_hidden, scaled, gate_grad, up_grad)


def gradient_rows(key_in, terms):
    key_hidden, scaled, gate_grad, up_grad = terms
    across = (((0,), (0,)), ((), ()))
    gate_rows = lax.dot_general(key_in, gate_grad, across, preferred_element_type=jnp.float32)
    up_rows = lax.dot_general(key_in, up_grad, across, preferred_element_type=jnp.float32)
    down_rows = lax.dot_general(key_hidden, scaled, across, preferred_element_type=jnp.float32)
    return jnp.stack([gate_rows, up_rows, down_rows], axis=1)


def renormed(previous, gradient):
    earlier = previous.astype(jnp.float32)
    updated = earlier + gradient
    factor = jnp.sqrt(jnp.mean(earlier * earlier, axis=-1, keepdims=True) + EPSILON) * lax.rsqrt(
        jnp.mean(updated * updated, axis=-1, keepdims=True) + EPSILON
    )
    return (updated * factor).astype(jnp.bfloat16)


def normalized(raw, gain_row):
    factor = lax.rsqrt(jnp.mean(raw * raw, axis=-1, keepdims=True) + EPSILON)
    return (raw * factor * gain_row).astype(jnp.bfloat16)


def attend(queries, key_block, value_block, allowed, head_size):
    tokens = queries.shape[0]
    per_head = queries.reshape(tokens, -1, head_size)
    scores = jnp.einsum(
        "qhd,kd->hqk", per_head, key_block, preferred_element_type=jnp.float32
    ) / math.sqrt(head_size)
    scores = jnp.where(allowed[None], scores, -1e30)
    row_max = jnp.max(scores, axis=-1, keepdims=True)
    lifted = jnp.exp(scores - row_max)
    weights = (lifted / jnp.sum(lifted, axis=-1, keepdims=True)).astype(jnp.bfloat16)
    mixed = jnp.einsum("hqk,kd->qhd", weights, value_block, preferred_element_type=jnp.float32)
    return mixed.reshape(tokens, -1)


def shards(fast_query, fast_key, fast_value, fast_rate, fast_weights, norm_gain, key_value):
    tokens = fast_query.shape[1]
    head_size = key_value.shape[2]
    place = lax.axis_index("tok")
    block_len = tokens * lax.axis_size("tok")
    own_rows = fast_weights[0]
    initial = lax.all_gather(own_rows, "tok", axis=0, tiled=True)
    terms = backward_terms(fast_key[0], fast_value[0], fast_rate[0], initial)
    gradient = lax.psum(gradient_rows(fast_key[0], terms), "tok")
    refreshed = renormed(initial, gradient)
    partner = from_partner(key_value, "head", 0)
    holds_key = lax.axis_index("head") % 2 == 0
    key_part = jnp.where(holds_key, key_value, partner)
    value_part = jnp.where(holds_key, partner, key_value)
    pair_stack = jnp.stack([key_part, value_part])
    reach = WIN // tokens
    arrived = []
    for distance in range(1, reach + 1):
        arrived.append(passed_along(pair_stack, "tok", distance))
    aligned = []
    for distance in range(reach, 0, -1):
        piece = arrived[distance - 1]
        aligned.append(jnp.where(place >= distance, piece, piece[:, 0:1]))
    aligned.append(pair_stack)
    window = jnp.concatenate(aligned, axis=2)
    span = window.shape[2]
    query_pos = lax.broadcasted_iota(jnp.int32, (tokens, span), 0)
    key_pos = lax.broadcasted_iota(jnp.int32, (tokens, span), 1) - reach * tokens
    offset = query_pos - key_pos
    inside = (offset >= 0) & (offset < WIN)

    def finish(block_index, matrices):
        fast_out = normalized(fast_apply(fast_query[block_index], matrices), norm_gain)
        allowed = inside & (block_index * block_len + place * tokens + key_pos >= 0)
        attended = attend(
            fast_out, window[0, block_index], window[1, block_index], allowed, head_size
        )
        return (fast_out.astype(jnp.float32) + attended).astype(jnp.bfloat16)

    first_final = finish(0, initial)
    second_final = finish(1, refreshed)
    return jnp.stack([first_final, second_final])

MESH = pl.DeviceIdType.MESH
ALONG_ROWS = (((0,), (0,)), ((), ()))
ALONG_COLUMNS = (((1,), (1,)), ((), ()))


def dot_along(left, right, dims):
    return lax.dot_general(left, right, dims, preferred_element_type=jnp.float32)


def mixed_heads(fast_out, keys, values, valid):
    tokens = fast_out.shape[0]
    size = keys[0].shape[1]
    heads = fast_out.shape[1] // size
    stacked = jnp.concatenate([fast_out[:, h * size : (h + 1) * size] for h in range(heads)], axis=0)
    scale = math.log2(math.e) / math.sqrt(size)
    scores = [dot_along(stacked, part, ALONG_COLUMNS) for part in keys]
    pieces = []
    for h in range(heads):
        masked = [
            jnp.where(ok, s[h * tokens : (h + 1) * tokens], -1e30) for s, ok in zip(scores, valid)
        ]
        top = jnp.max(masked[0], axis=-1, keepdims=True)
        for more in masked[1:]:
            top = jnp.maximum(top, jnp.max(more, axis=-1, keepdims=True))
        lifted = [jnp.exp2((part - top) * scale) for part in masked]
        total = jnp.sum(lifted[0], axis=-1, keepdims=True)
        for more in lifted[1:]:
            total = total + jnp.sum(more, axis=-1, keepdims=True)
        inverse = 1.0 / total
        pieces.append([(part * inverse).astype(jnp.bfloat16) for part in lifted])
    mixed = None
    for i, part in enumerate(values):
        weights = jnp.concatenate([piece[i] for piece in pieces], axis=0)
        term = product(weights, part)
        mixed = term if mixed is None else mixed + term
    return jnp.concatenate([mixed[h * tokens : (h + 1) * tokens] for h in range(heads)], axis=1)


def whole_kernel(
    query_ref, key_ref, value_ref, rate_ref, weight_ref, gain_ref, kv_ref, out_ref,
    w_buf, k_buf, s_buf, kv_buf, hidden_buf, gates_buf, new_buf, merged, grad_buf,
    send_sem, recv_sem, z_send, z_recv,
):
    me = lax.axis_index("tok")
    head = lax.axis_index("head")
    kind = lax.rem(head, 2)
    core = lax.rem(me, 2)
    first_hop = jnp.where(core == 0, 2, 4)
    second_hop = 6 - first_hop
    sibling = me ^ 1
    near, far = me ^ first_hop, me ^ second_hop
    opposite = me ^ 6
    opposite_head = head ^ 1
    barrier = pltpu.get_barrier_semaphore()
    for there in (sibling, near, far):
        pl.semaphore_signal(barrier, inc=1, device_id=(there, head), device_id_type=MESH)
    pl.semaphore_signal(barrier, inc=1, device_id=(me, opposite_head), device_id_type=MESH)

    tokens = key_ref.shape[1]
    parts, depth, _ = weight_ref.shape
    hd = key_ref.shape[2]
    size = kv_ref.shape[2]

    def rows(owner, count):
        return pl.ds(pl.multiple_of(owner * count, count), count)

    own = rows(me, tokens)
    for part in range(parts):
        w_buf[rows(me, depth), part * hd : (part + 1) * hd] = weight_ref[part]
    k_buf[own] = key_ref[0]
    rates = jnp.broadcast_to(rate_ref[0], (tokens, tokens)).T[:, :1]
    s_buf[own] = (rates * value_ref[0].astype(jnp.float32)).astype(jnp.bfloat16)
    kv_buf[kind, :, own] = kv_ref[...]

    def part_of(item, owner):
        if item == 0:
            return w_buf.at[rows(owner, depth)]
        if item == 1:
            return kv_buf.at[kind, :, rows(owner, tokens)]
        if item == 2:
            return k_buf.at[rows(owner, tokens)]
        if item == 3:
            return s_buf.at[rows(owner, tokens)]
        return kv_buf.at[1 - kind, :, rows(owner, tokens)]

    owners = [
        me, near, far, opposite,
        sibling, sibling ^ 2, sibling ^ 4, sibling ^ 6,
    ]
    started = []

    def send(item, source, target, slot):
        number = len(started)
        copy = pltpu.make_async_remote_copy(
            src_ref=part_of(item, owners[source]),
            dst_ref=part_of(item, owners[source]),
            send_sem=send_sem.at[number],
            recv_sem=recv_sem.at[item, slot],
            device_id=(target, head),
            device_id_type=MESH,
        )
        copy.start()
        started.append(copy)

    across = []

    def send_across(source):
        ref = part_of(1, owners[source])
        copy = pltpu.make_async_remote_copy(
            src_ref=ref, dst_ref=ref, send_sem=z_send.at[source], recv_sem=z_recv.at[source],
            device_id=(me, opposite_head), device_id_type=MESH,
        )
        copy.start()
        across.append(copy)

    def arrived(item, slot):
        ref = part_of(item, owners[slot])
        pltpu.make_async_remote_copy(
            src_ref=ref, dst_ref=ref, send_sem=send_sem.at[0], recv_sem=recv_sem.at[item, slot],
            device_id=(sibling, head), device_id_type=MESH,
        ).wait_recv()

    def arrived_across(source):
        ref = part_of(4, owners[source])
        pltpu.make_async_remote_copy(
            src_ref=ref, dst_ref=ref, send_sem=z_send.at[0], recv_sem=z_recv.at[source],
            device_id=(me, opposite_head), device_id_type=MESH,
        ).wait_recv()

    side = {0: 4, 1: jnp.where(core == 0, 5, 6), 2: jnp.where(core == 0, 6, 5), 3: 7}

    def to_sibling(item, source):
        send(item, source, sibling, side[source])

    def pass_on(item, source):
        arrived(item, source)
        if source == 1:
            send(item, 1, far, 3)
        to_sibling(item, source)

    pl.semaphore_wait(barrier, 4)
    for item in range(4):
        send(item, 0, near, 1)
    for item in range(2):
        send(item, 0, far, 2)
    for item in range(4):
        to_sibling(item, 0)
    send_across(0)
    for item in range(4):
        pass_on(item, 1)
        if item < 2:
            send(item + 2, 0, far, 2)
        if item == 1:
            send_across(1)
    pass_on(0, 2)
    pass_on(1, 2)
    send_across(2)
    pass_on(2, 2)
    pass_on(0, 3)
    for slot in range(4, 8):
        arrived(0, slot)

    gain = gain_ref[...]

    def rms(total):
        return lax.rsqrt(jnp.mean(total * total, axis=-1, keepdims=True) + EPSILON)

    def applied(block, buf):
        both = product(query_ref[block], buf[:, : 2 * hd])
        gate_value, up_value = both[:, :hd], both[:, hd:]
        hidden = (jax.nn.silu(gate_value) * up_value).astype(jnp.bfloat16)
        raw = product(hidden, buf[:, 2 * hd :])
        return (raw * rms(raw) * gain).astype(jnp.bfloat16)

    fast_first = applied(0, w_buf)

    def terms(chip):
        span = rows(chip, 2 * tokens)
        both = product(k_buf[span], w_buf[:, : 2 * hd])
        gate_value, up_value = both[:, :hd], both[:, hd:]
        sig = jax.nn.sigmoid(gate_value)
        act = gate_value * sig
        hidden_buf[span] = (act * up_value).astype(jnp.bfloat16)
        backward = dot_along(s_buf[span], w_buf[:, 2 * hd :], ALONG_COLUMNS)
        gates_buf[span, :hd] = (
            backward * up_value * sig * (1.0 + gate_value * (1.0 - sig))
        ).astype(jnp.bfloat16)
        gates_buf[span, hd:] = (backward * act).astype(jnp.bfloat16)

    def gradient(chip):
        span = rows(chip, 2 * tokens)
        both = dot_along(k_buf[span], gates_buf[span], ALONG_ROWS)
        down = dot_along(hidden_buf[span], s_buf[span], ALONG_ROWS)
        return both, down

    def accumulate(chip, first=False):
        both, down = gradient(chip)
        grad_buf[:, : 2 * hd] = both if first else grad_buf[:, : 2 * hd] + both
        grad_buf[:, 2 * hd :] = down if first else grad_buf[:, 2 * hd :] + down

    chip = me // 2
    arrived(2, 4)
    arrived(3, 4)
    terms(chip)
    pass_on(3, 2)
    accumulate(chip, first=True)
    pass_on(1, 3)
    send_across(3)
    for source in range(4):
        arrived_across(source)
        to_sibling(4, source)
    for slot in (5, 6):
        arrived(2, slot)
        arrived(3, slot)
    terms(chip ^ 1)
    accumulate(chip ^ 1)
    terms(chip ^ 2)
    accumulate(chip ^ 2)
    for slot in range(4, 8):
        arrived(1, slot)
        arrived(4, slot)
    pass_on(2, 3)
    pass_on(3, 3)

    length = k_buf.shape[0]
    query_pos = me * tokens + lax.broadcasted_iota(jnp.int32, (tokens, length), 0)
    key_pos = lax.broadcasted_iota(jnp.int32, (tokens, length), 1)
    mixed = mixed_heads(fast_first, [kv_buf[0, 0]], [kv_buf[1, 0]], [key_pos <= query_pos])
    out_ref[0] = (fast_first.astype(jnp.float32) + mixed).astype(jnp.bfloat16)

    arrived(2, 7)
    arrived(3, 7)
    terms(chip ^ 3)

    def renewed(part, gradient):
        columns = slice(part * hd, (part + 1) * hd)
        earlier = w_buf[:, columns].astype(jnp.float32)
        updated = earlier + gradient
        factor = jnp.sqrt(jnp.mean(earlier * earlier, axis=-1, keepdims=True) + EPSILON) * rms(updated)
        new_buf[:, columns] = (updated * factor).astype(jnp.bfloat16)

    both, down = gradient(chip ^ 3)
    renewed(0, grad_buf[:, :hd] + both[:, :hd])
    renewed(1, grad_buf[:, hd : 2 * hd] + both[:, hd:])
    renewed(2, grad_buf[:, 2 * hd :] + down)

    fast_second = applied(1, new_buf)
    for shard in range(length // tokens):
        place = slice(shard * tokens, (shard + 1) * tokens)
        block = jnp.where(shard < me, 1, 0)
        merged[0, place] = kv_buf[0, block, place]
        merged[1, place] = kv_buf[1, block, place]
    near_query = lax.broadcasted_iota(jnp.int32, (tokens, tokens), 0)
    near_key = lax.broadcasted_iota(jnp.int32, (tokens, tokens), 1)
    mixed = mixed_heads(
        fast_second,
        [merged[0], kv_buf[0, 1, own]],
        [merged[1], kv_buf[1, 1, own]],
        [(key_pos < me * tokens) | (key_pos > query_pos), near_key <= near_query],
    )
    out_ref[1] = (fast_second.astype(jnp.float32) + mixed).astype(jnp.bfloat16)
    for copy in started + across:
        copy.wait_send()


def gathered_shards(fast_query, fast_key, fast_value, fast_rate, fast_weights, norm_gain, key_value):
    members = lax.axis_size("tok")
    _, depth, parts, hd = fast_weights.shape
    _, tokens, size = key_value.shape
    length = members * tokens
    weights = jnp.swapaxes(fast_weights[0], 0, 1)
    rates = jnp.swapaxes(fast_rate, 1, 2)
    sends = 4 * (members - 1) + members // 2
    bf16 = jnp.bfloat16
    return pl.pallas_call(
        whole_kernel,
        out_shape=jax.ShapeDtypeStruct(fast_query.shape, bf16),
        in_specs=[pl.BlockSpec(memory_space=pltpu.VMEM)] * 7,
        out_specs=pl.BlockSpec(memory_space=pltpu.VMEM),
        scratch_shapes=[
            pltpu.VMEM((members * depth, parts * hd), bf16),
            pltpu.VMEM((length, hd), bf16),
            pltpu.VMEM((length, hd), bf16),
            pltpu.VMEM((2, 2, length, size), bf16),
            pltpu.VMEM((length, hd), bf16),
            pltpu.VMEM((length, 2 * hd), bf16),
            pltpu.VMEM((members * depth, parts * hd), bf16),
            pltpu.VMEM((2, length, size), bf16),
            pltpu.VMEM((members * depth, parts * hd), jnp.float32),
            pltpu.SemaphoreType.DMA((sends,)),
            pltpu.SemaphoreType.DMA((5, members)),
            pltpu.SemaphoreType.DMA((members // 2,)),
            pltpu.SemaphoreType.DMA((members // 2,)),
        ],
        compiler_params=pltpu.CompilerParams(
            collective_id=0, has_side_effects=True, vmem_limit_bytes=60 * 1024 * 1024
        ),
    )(fast_query, fast_key, fast_value, rates, weights, norm_gain[None], key_value)


def solution(mesh):
    in_specs = (
        P(None, "tok", "head"),
        P(None, "tok", "head"),
        P(None, "tok", "head"),
        P(None, "tok", "head"),
        P("head", "tok", None, None),
        P("head"),
        P(None, "tok", "head"),
    )
    out_specs = P(None, "tok", "head")
    plan = gathered_shards if mesh.shape["tok"] == 8 else shards
    return jax.shard_map(plan, mesh=mesh, in_specs=in_specs, out_specs=out_specs, check_vma=False)
```
